32 devices in a mesh: pipe: 4 (over y, core), expert: 8 (over z, x).
Axes of the slice: x: 2, y: 2, z: 4, core: 2. Of those that a mesh axis runs over, the one named last changes fastest.
Arguments:
- saved_inputs: bfloat16 [4, 1024, 2048], P('pipe', 'expert'), may hold values from -6 to 6
- grad_out: bfloat16 [4, 1024, 2048], P('pipe', 'expert'), may hold values from -6 to 6
- routes: int32 [4, 1024, 8], P('pipe', 'expert'), may hold values from 0 to 31, all different within a row; in each aligned block of 128 rows (0 to 127, 128 to 255, ..., all dimensions but the last counted through in order) at most 36 rows name the same one
- route_probs: float32 [4, 1024, 8], P('pipe', 'expert'), may hold values from 0.1 to 0.6
- w_in: bfloat16 [4, 32, 2048, 768], P('pipe', 'expert'), may hold values from -0.125 to 0.125
- w_out: bfloat16 [4, 32, 384, 2048], P('pipe', 'expert'), may hold values from -0.3125 to 0.3125
Outputs:
- grad_tokens: float32 [4, 1024, 2048], P('pipe', 'expert')
- grad_w_in: bfloat16 [4, 32, 2048, 768], P('pipe', 'expert')
- grad_w_out: bfloat16 [4, 32, 384, 2048], P('pipe', 'expert')
The draws below stay inside these ranges and needn't reach their ends.
Inputs may be any that keep to these rules, and one draw needn't show every extreme that they name: `routes`: each row names 8 different experts. Among the rows of one device (aligned blocks of 128 rows) no expert is named more than 36 times, a bound that some block reaches.
All inputs are finite; a program needn't handle non-finite values.
Results may differ from the reference program's by a relative error of at most 0.0057.
Values may be sent and summed in bfloat16 or wider, within the bound.
A program may use at most 128 MiB of HBM per device.

```python
import math
import jax
import jax.numpy as jnp
import numpy as np
from jax import lax

D = 2048
FF = 384
TOP = 8
EXPERTS = 32
TOK_DEV = 128
CAP = 36
TOKENS = 1024
N_PIPE = 4
N_EXPERT = 8


def shard_levels(key, extent, cuts, low, top_value):
    factor_of = 1.0
    for dim, parts in cuts:
        draws = jax.random.uniform(jax.random.fold_in(jax.random.fold_in(key, 6), dim), (parts,), jnp.float32, low / len(cuts), top_value / len(cuts))
        factor_of = factor_of * jnp.repeat(jnp.exp(draws), extent[dim] // parts).reshape((-1,) + (1,) * (len(extent) - 1 - dim))
    return factor_of


def shared_out(stream_key, own, number, rows, amount, top, most, skew):
    sequence = jax.random.permutation(stream_key, amount)
    crowded, ordinary = load_shares(amount, rows * top, most, skew, True), load_shares(amount, rows * top, most, skew, False)
    places = jnp.arange(amount)

    def named(sizes, rotation):
        used = int((sizes > 0).sum())
        fixed = max(1, used // 4)
        moved = fixed + (places - fixed + rotation * (used - fixed)) % max(1, amount - fixed)
        return jnp.zeros((amount,), jnp.int32).at[sequence[jnp.where(places < fixed, places, moved)]].set(jnp.asarray(sizes, jnp.int32))

    sizes = jnp.where(number % 4 == 0, named(crowded, number // 4), named(ordinary, number - number // 4 - 1))
    mixed = jax.random.permutation(jax.random.fold_in(own, 3), amount)
    donor, taker = mixed[0:amount // 2 * 2:2], mixed[1:amount // 2 * 2:2]
    margin = jnp.minimum(sizes[donor] - 1, most - sizes[taker]) // 2
    margin = jnp.where((donor == sequence[0]) | (taker == sequence[0]) | (sizes[taker] == 0), 0, jnp.maximum(margin, 0))
    moved = jax.random.randint(jax.random.fold_in(own, 4), (amount // 2,), 0, 1 << 20) % (margin + 1)
    sizes = sizes.at[donor].add(-moved).at[taker].add(moved)
    labels = jnp.searchsorted(jnp.cumsum(sizes), jnp.arange(rows * top), side="right").astype(jnp.int32)
    grid = labels.reshape(top, rows).T
    grid = grid[jax.random.permutation(jax.random.fold_in(own, 1), rows)]
    rotation = jax.random.randint(jax.random.fold_in(own, 2), (rows, 1), 0, top)
    return jnp.take_along_axis(grid, (jnp.arange(top)[None, :] + rotation) % top, axis=1)


def load_shares(amount, total, limit, lean, full):
    portions = [(1 << 20) // math.isqrt(standing ** lean) + 1 for standing in range(1, amount + 1)]
    largest = limit if full else min(limit, max(-(-total // amount), total * portions[0] // sum(portions)))
    least = 1 if total - largest >= amount - 1 else 0
    holding, rest = [largest] + [least] * (amount - 1), total - largest - least * (amount - 1)
    while rest > 0:
        candidates = [i for i in range(1, amount) if holding[i] < largest] or [i for i in range(1, amount) if holding[i] < limit]
        mass, left = sum([portions[i] for i in candidates]), rest
        for i in candidates:
            more = min(limit - holding[i], max(1, left * portions[i] // mass), rest)
            holding[i] = holding[i] + more
            rest = rest - more
    return np.array(holding)


def normal_values(rng, shape, spread, bound, shards=(), kind=jnp.bfloat16):
    factor_of = shard_levels(rng, shape, shards, -0.22, 0.18) if shards else 1.0
    entries = jax.random.normal(rng, shape, jnp.float32) * spread * factor_of
    return jnp.minimum(jnp.maximum(entries, -bound), bound).astype(kind)


def setup_inputs(seed: int = 0) -> dict:
    arg_keys = jax.random.split(jax.random.key(seed), 7)
    saved_inputs = normal_values(arg_keys[0], (N_PIPE, TOKENS, D), 1.0, 6.0, ((0, 4), (1, 8)))
    grad_out = normal_values(arg_keys[1], (N_PIPE, TOKENS, D), 1.0, 6.0, ((0, 4), (1, 8)))
    routes_keys = jax.random.split(jax.random.fold_in(arg_keys[2], 1), N_PIPE * TOKENS // TOK_DEV)
    routes_turns = jax.random.permutation(jax.random.fold_in(arg_keys[2], 3), N_PIPE * TOKENS // TOK_DEV)
    routes = jax.vmap(lambda own, number: shared_out(jax.random.fold_in(arg_keys[2], 2), own, number, TOK_DEV, EXPERTS, TOP, CAP, 2))(routes_keys, routes_turns).reshape((N_PIPE, TOKENS, TOP))
    route_probs = jnp.clip(0.1 + 0.5 * jax.random.uniform(arg_keys[3], (N_PIPE, TOKENS, TOP), jnp.float32) ** shard_levels(arg_keys[3], (N_PIPE, TOKENS, TOP), ((0, 4), (1, 8)), -0.2, 0.2), 0.1, 0.6)
    w_in = normal_values(arg_keys[4], (N_PIPE, EXPERTS, D, 2 * FF), D ** -0.5, 0.125, ((0, 4), (1, 8)))
    w_out = normal_values(arg_keys[5], (N_PIPE, EXPERTS, FF, D), FF ** -0.5, 0.3125, ((0, 4), (1, 8)))
    return dict(saved_inputs=saved_inputs, grad_out=grad_out, routes=routes, route_probs=route_probs, w_in=w_in, w_out=w_out)


def silu_parts(gates):
    sigma = jax.nn.sigmoid(gates)
    return gates * sigma, sigma * (1.0 + gates * (1.0 - sigma))


def slot_table(route_ids, route_weights, first, count, capacity):
    tok_count, top_count = route_ids.shape
    flat_ids = route_ids.reshape(-1)
    expert_ids = first + jnp.arange(count, dtype=jnp.int32)
    onehot = (flat_ids[:, None] == expert_ids[None, :]).astype(jnp.int32)
    ranks = jnp.cumsum(onehot, axis=0) - 1
    slots = jnp.sum(onehot * ranks, axis=1)
    local_ids = jnp.sum(onehot * jnp.arange(count, dtype=jnp.int32)[None, :], axis=1)
    hits = jnp.sum(onehot, axis=1)
    dest = jnp.where(hits > 0, local_ids * capacity + slots, count * capacity).astype(jnp.int32)
    token_ids = (jnp.arange(tok_count * top_count, dtype=jnp.int32) // top_count).astype(jnp.int32)
    table = jnp.full((count * capacity + 1,), -1, jnp.int32).at[dest].set(token_ids)[: count * capacity]
    weight = jnp.zeros((count * capacity + 1,), jnp.float32).at[dest].set(route_weights.reshape(-1).astype(jnp.float32))[: count * capacity]
    return table, weight, dest


def pick_rows(input_rows, grad_rows, table, weight):
    valid = table >= 0
    safe_index = jnp.maximum(table, 0)
    picked = jnp.where(valid[:, None], input_rows[safe_index], jnp.zeros((), input_rows.dtype))
    scaled = (weight[:, None] * grad_rows[safe_index].astype(jnp.float32)).astype(jnp.bfloat16)
    return picked, scaled


def expert_grads(expert_in, expert_grad, weight_in, weight_out):
    hidden_units = weight_out.shape[0]
    gate_up = jnp.dot(expert_in, weight_in, preferred_element_type=jnp.float32)
    gates = gate_up[:, :hidden_units]
    upper = gate_up[:, hidden_units:]
    active, slope = silu_parts(gates)
    hidden = (active * upper).astype(jnp.bfloat16)
    hidden_grad = jnp.dot(expert_grad, weight_out.T, preferred_element_type=jnp.float32)
    pre_grad = jnp.concatenate([hidden_grad * upper * slope, hidden_grad * active], axis=1).astype(jnp.bfloat16)
    grad_out_w = jnp.dot(hidden.T, expert_grad, preferred_element_type=jnp.float32).astype(jnp.bfloat16)
    grad_in_w = jnp.dot(expert_in.T, pre_grad, preferred_element_type=jnp.float32).astype(jnp.bfloat16)
    row_grads = jnp.dot(pre_grad, weight_in.T, preferred_element_type=jnp.float32).astype(jnp.bfloat16)
    return row_grads, grad_in_w, grad_out_w


def combine_rows(buffer_rows, dest):
    gathered = buffer_rows[dest].astype(jnp.float32).reshape(-1, TOP, buffer_rows.shape[1])
    return jnp.sum(gathered, axis=1)


def one_section(packed):
    section_in, section_grad, section_routes, section_probs, weight_in, weight_out = packed
    block_in = section_in.reshape(N_EXPERT, TOK_DEV, D)
    block_grad = section_grad.reshape(N_EXPERT, TOK_DEV, D)
    tables, weights, dests = jax.vmap(lambda ids, probs: slot_table(ids, probs, 0, EXPERTS, CAP))(
        section_routes.reshape(N_EXPERT, TOK_DEV, TOP), section_probs.reshape(N_EXPERT, TOK_DEV, TOP))
    rows_in, rows_grad = jax.vmap(pick_rows)(block_in, block_grad, tables, weights)
    rows_in = rows_in.reshape(N_EXPERT, EXPERTS, CAP, D).transpose(1, 0, 2, 3).reshape(EXPERTS, N_EXPERT * CAP, D)
    rows_grad = rows_grad.reshape(N_EXPERT, EXPERTS, CAP, D).transpose(1, 0, 2, 3).reshape(EXPERTS, N_EXPERT * CAP, D)
    row_grads, grad_in_w, grad_out_w = lax.map(lambda items: expert_grads(*items), (rows_in, rows_grad, weight_in, weight_out))
    row_grads = row_grads.reshape(EXPERTS, N_EXPERT, CAP, D).transpose(1, 0, 2, 3).reshape(N_EXPERT, EXPERTS * CAP, D)
    token_grads = jax.vmap(combine_rows)(row_grads, dests)
    return token_grads.reshape(TOKENS, D), grad_in_w, grad_out_w


def reference(saved_inputs, grad_out, routes, route_probs, w_in, w_out):
    section_inputs = saved_inputs[::-1]
    grad_tokens, grad_w_in, grad_w_out = lax.map(one_section, (section_inputs, grad_out, routes, route_probs, w_in, w_out))
    return grad_tokens, grad_w_in, grad_w_out
```

```python
import jax
import jax.numpy as jnp
from jax import lax
from jax.sharding import PartitionSpec as P

CAP = 36


def swapped(block, axis):
    count = lax.axis_size(axis)
    return lax.ppermute(block, axis, [(i, count - 1 - i) for i in range(count)])


def silu_parts(gates):
    sigma = jax.nn.sigmoid(gates)
    return (gates * sigma, sigma * (1.0 + gates * (1.0 - sigma)))


def picks(meta, first, count, capacity, top):
    ids, probs = meta[..., :top], meta[..., top:]
    experts = (first + jnp.arange(count)).astype(jnp.float32)
    named = ids[:, None] == experts[None, :, None, None]
    hit = jnp.any(named, axis=-1)
    weight = jnp.sum(jnp.where(named, probs[:, None], 0.0), axis=-1)
    tokens = jnp.arange(ids.shape[1])
    earlier = (tokens[:, None] < tokens[None, :]).astype(jnp.bfloat16)
    rank = jnp.einsum("set,tu->seu", hit.astype(jnp.bfloat16), earlier, preferred_element_type=jnp.float32)
    slot = jnp.arange(capacity).astype(jnp.float32)
    pick = hit[:, :, None, :] & (rank[:, :, None, :] == slot[None, None, :, None])
    row_weight = jnp.sum(jnp.where(pick, weight[:, :, None, :], 0.0), axis=-1)
    return pick.astype(jnp.bfloat16), row_weight


def plain(saved_inputs, grad_out, routes, route_probs, w_in, w_out):
    owner_count = lax.axis_size("expert")
    weight_in, weight_out = w_in[0], w_out[0]
    local_experts, width, hidden2 = weight_in.shape
    hidden_units = hidden2 // 2
    tok_count, top = routes.shape[1:]
    meta = jnp.concatenate([routes[0].astype(jnp.float32), route_probs[0]], axis=1)
    every_meta = lax.all_gather(meta, "expert", axis=0)
    section_in = swapped(saved_inputs[0], "pipe")
    every_grad = lax.all_gather(grad_out[0], "expert", axis=0)
    every_in = lax.all_gather(section_in, "expert", axis=0)
    first = lax.axis_index("expert") * local_experts
    pick, row_weight = picks(every_meta, first, local_experts, CAP, top)
    f32 = jnp.float32
    rows_in = jnp.einsum("sect,std->secd", pick, every_in, preferred_element_type=f32).astype(jnp.bfloat16)
    rows_grad = jnp.einsum("sect,std->secd", pick, every_grad, preferred_element_type=f32)
    rows_grad = (rows_grad * row_weight[..., None]).astype(jnp.bfloat16)
    gate_up = jnp.einsum("secd,edf->secf", rows_in, weight_in, preferred_element_type=f32)
    gates, upper = gate_up[..., :hidden_units], gate_up[..., hidden_units:]
    active, slope = silu_parts(gates)
    hidden = (active * upper).astype(jnp.bfloat16)
    hidden_grad = jnp.einsum("secd,efd->secf", rows_grad, weight_out, preferred_element_type=f32)
    pre_grad = jnp.concatenate([hidden_grad * upper * slope, hidden_grad * active], axis=3).astype(jnp.bfloat16)
    row_grads = jnp.einsum("secf,edf->secd", pre_grad, weight_in, preferred_element_type=f32).astype(jnp.bfloat16)
    partial = jnp.einsum("sect,secd->std", pick, row_grads, preferred_element_type=f32).astype(jnp.bfloat16)
    back = lax.all_to_all(partial, "expert", split_axis=0, concat_axis=0, tiled=True)
    grad_out_w = jnp.einsum("secf,secd->efd", hidden, rows_grad, preferred_element_type=f32).astype(jnp.bfloat16)
    grad_in_w = jnp.einsum("secd,secf->edf", rows_in, pre_grad, preferred_element_type=f32).astype(jnp.bfloat16)
    token_grads = jnp.sum(back.astype(f32), axis=0)
    return (token_grads[None], grad_in_w[None], grad_out_w[None])


def solution(mesh):
    rows = P("pipe", "expert", None)
    weights = P("pipe", "expert", None, None)
    return jax.shard_map(
        plain, mesh=mesh, in_specs=(rows, rows, rows, rows, weights, weights),
        out_specs=(rows, weights, weights), check_vma=False,
    )
```
